128 devices in a mesh: dp: 64 (over y, x, z_lo, core), mp: 2 (over z_hi).
Axes of the slice: x: 4, y: 4, z: 4 (z_hi: 2, z_lo: 2; z = z_hi * 2 + z_lo), core: 2. Of those that a mesh axis runs over, the one named last changes fastest.
Arguments:
- activations: bfloat16 [131072, 2048], P('dp'), may hold values from -400 to 400
- out_grads: bfloat16 [131072, 4096], P('dp', 'mp'), may hold values from -400 to 400
- old_basis: bfloat16 [3, 2048, 256], replicated, may hold values from -0.125 to 0.125
- old_eigen: float32 [3, 256], replicated, may hold values from 0.5 to 40
- flags: int32 [3], replicated, may hold values from 0 to 1, as said below
Outputs:
- preconditioned: float32 [2048, 4096], P('dp', 'mp')
The draws below stay inside these ranges and needn't reach their ends.
Inputs may be any that keep to these rules, and one draw needn't show every extreme that they name: `flags`: at least one block is flagged and at least one is not.
All inputs are finite; a program needn't handle non-finite values.
Results may differ from the reference program's by a relative error of at most 0.0025.
Values may be sent and summed in bfloat16 or wider, within the bound.
No kernel may reach another device: no remote copies, remote signals or barrier semaphores. Data moves between devices by JAX's collectives and lax.ppermute only.
A program may use at most 128 MiB of HBM per device.

```python
import math
import jax
import jax.numpy as jnp
from jax import lax

BS = 2048
RANK = 256
TOKENS = 131072
GCOLS = 4096
BLOCKS = 3
N_MP = 2


def shape_rows(key, base, spread):
    rows, cols = base.shape
    key_chan, key_tok = jax.random.split(key, 2)
    channel = jnp.exp(jax.random.uniform(key_chan, (1, cols), jnp.float32, math.log(0.5), math.log(5.5)))
    position = jnp.arange(rows, dtype=jnp.float32) / rows
    token = jnp.exp(jax.random.uniform(key_tok, (rows, 1), jnp.float32, 0.0, math.log(spread)))
    token = token * jnp.exp(math.log(3.0) * position)[:, None]
    mixed = base
    return (mixed * token * channel).astype(jnp.bfloat16)


def draw_activations(key, part):
    key = jax.random.fold_in(key, 11)
    key_base, key_shape = jax.random.split(key)
    base = jnp.clip(jax.random.normal(key_base, (TOKENS, BS), jnp.float32), -4.0, 4.0)
    return shape_rows(key_shape, base, 1.0)


def draw_out_grads(key, part):
    key = jax.random.fold_in(key, 23)
    key_base, key_shape = jax.random.split(key)
    base = jnp.clip(jax.random.normal(key_base, (TOKENS, GCOLS), jnp.float32), -4.0, 4.0)
    return shape_rows(key_shape, base, 1.0)


def draw_flags(key, part):
    key = jax.random.fold_in(key, 37)
    key_bits, key_order = jax.random.split(key)
    bits = jax.random.randint(key_bits, (BLOCKS,), 0, 2).astype(jnp.int32)
    order = jax.random.permutation(key_order, BLOCKS).astype(jnp.int32)
    places = jnp.arange(BLOCKS, dtype=jnp.int32)
    bits = jnp.where(places == order[0], 1, bits)
    bits = jnp.where(places == order[1], 0, bits)
    return bits.astype(jnp.int32)


def gaussian(key, extent, scale, limit, kind=jnp.bfloat16):
    values = jax.random.normal(key, extent, jnp.float32) * scale
    return jnp.minimum(jnp.maximum(values, -limit), limit).astype(kind)


def setup_inputs(seed: int = 0) -> dict:
    streams_of = jax.random.split(jax.random.key(seed), 6)
    activations = draw_activations(jax.random.fold_in(streams_of[5], 71), 0)
    out_grads = draw_out_grads(jax.random.fold_in(streams_of[5], 71), 0)
    old_basis = gaussian(streams_of[2], (BLOCKS, BS, RANK), BS ** -0.5, 0.125)
    old_eigen = jnp.clip(jnp.exp(jax.random.uniform(streams_of[3], (BLOCKS, RANK), jnp.float32, math.log(0.5), math.log(40.0))), 0.5, 40.0)
    flags = draw_flags(jax.random.fold_in(streams_of[5], 71), 0)
    return dict(activations=activations, out_grads=out_grads, old_basis=old_basis, old_eigen=old_eigen, flags=flags)


def orthonormal(power):
    gram = jnp.einsum('ki,kj->ij', power, power, precision=lax.Precision.HIGHEST)
    chol = jnp.linalg.cholesky(gram)
    fresh = jax.scipy.linalg.solve_triangular(chol, power.T, lower=True).T
    return (fresh, jnp.diagonal(chol))

def reference(activations, out_grads, old_basis, old_eigen, flags):
    blocks = [activations] + [out_grads[:, m * BS:(m + 1) * BS] for m in range(N_MP)]
    bases = []
    eigens = []
    for index in range(len(blocks)):
        data = blocks[index]
        projected = jnp.dot(data.astype(jnp.float32), old_basis[index].astype(jnp.float32), preferred_element_type=jnp.float32).astype(jnp.bfloat16)
        power = jnp.dot(data.T.astype(jnp.float32), projected.astype(jnp.float32), preferred_element_type=jnp.float32) / TOKENS
        fresh, fresh_eig = orthonormal(power)
        chosen = jnp.where(flags[index] == 1, fresh, old_basis[index].astype(jnp.float32))
        bases.append(chosen.astype(jnp.bfloat16).astype(jnp.float32))
        eigens.append(jnp.where(flags[index] == 1, fresh_eig, old_eigen[index]))
    scale = 1.0 / math.sqrt(TOKENS)
    results = []
    for m in range(N_MP):
        grad = jnp.dot(activations.T.astype(jnp.float32), blocks[1 + m].astype(jnp.float32), preferred_element_type=jnp.float32) * scale
        right = jnp.dot(grad, bases[1 + m], precision=lax.Precision.HIGHEST)
        core = jnp.einsum('ki,kj->ij', bases[0], right, precision=lax.Precision.HIGHEST)
        damping = jnp.mean(eigens[0]) * jnp.mean(eigens[1 + m])
        outer = eigens[0][:, None] * eigens[1 + m][None, :]
        weight = outer / (outer + damping)
        left = jnp.dot(bases[0], weight * core, precision=lax.Precision.HIGHEST)
        correction = jnp.einsum('ir,kr->ik', left, bases[1 + m], precision=lax.Precision.HIGHEST)
        results.append(grad - correction)
    return jnp.concatenate(results, axis=1)
```

```python
import functools
import math

import jax
import jax.numpy as jnp
from jax import lax
from jax.experimental import pallas as pl
from jax.experimental.pallas import tpu as pltpu
from jax.sharding import Mesh, PartitionSpec as P

DP = ("y", "x", "z", "c")
CHIPS = ("y", "x", "z")
HIGHEST = lax.Precision.HIGHEST
TOP = (((0,), (0,)), ((), ()))
LAST = (((1,), (1,)), ((), ()))
BLK = 32
SUB = 8
EDGE = 8
VMEM_BYTES = 50 << 20
BRIEF = pl.CostEstimate(flops=1_000_000, bytes_accessed=10_000, transcendentals=0)


def small_factor(cols):
    shape = cols[0].shape
    e = [[jnp.broadcast_to(cols[k][i:i + 1, :], shape) for k in range(i + 1)] for i in range(SUB)]
    low = [[None] * SUB for _ in range(SUB)]
    rinv = []
    for j in range(SUB):
        d = e[j][j]
        r = lax.rsqrt(d)
        r = r * (1.5 - 0.5 * d * r * r)
        rinv.append(r)
        for i in range(j + 1, SUB):
            low[i][j] = e[i][j] * r
        for i in range(j + 1, SUB):
            for k in range(j + 1, i + 1):
                e[i][k] = e[i][k] - low[i][j] * low[k][j]
    inv = [[None] * SUB for _ in range(SUB)]
    for k in range(SUB):
        inv[k][k] = rinv[k]
        for i in range(k + 1, SUB):
            s = low[i][k] * inv[k][k]
            for m in range(k + 1, i):
                s = s + low[i][m] * inv[m][k]
            inv[i][k] = -s * rinv[i]
    return inv


def lane_splat(x, col):
    return jnp.broadcast_to(x[:, col:col + 1], (SUB, 128))


def rows_times(coefs, rows):
    n = rows.shape[1]
    out = []
    for g in range(n // 128):
        t = rows[:, g * 128:(g + 1) * 128]
        prods = [coefs[k] * jnp.broadcast_to(t[k:k + 1, :], (SUB, 128)) for k in range(SUB)]
        while len(prods) > 1:
            prods = [a + b for a, b in zip(prods[::2], prods[1::2])]
        out.append(prods[0])
    return jnp.concatenate(out, axis=1)


def factor_steps(m_ref, u_ref):
    n = m_ref.shape[0]
    sub = lax.broadcasted_iota(jnp.int32, (SUB, 128), 0)
    for r0 in range(0, n, BLK):
        panels = [m_ref[r0 + SUB * p:r0 + SUB * (p + 1), :] for p in range(BLK // SUB)]
        for p in range(BLK // SUB):
            c0 = r0 + SUB * p
            inv = small_factor([lane_splat(panels[p], c0 + m) for m in range(SUB)])
            coefs = []
            for k in range(SUB):
                v = jnp.zeros((SUB, 128), jnp.float32)
                for i in range(k, SUB):
                    v = jnp.where(sub == i, inv[i][k], v)
                coefs.append(v)
            u = rows_times(coefs, panels[p])
            u_ref[c0:c0 + SUB, :] = u
            for q in range(p + 1, BLK // SUB):
                cols = [lane_splat(panels[q], c0 + m) for m in range(SUB)]
                cq = []
                for k in range(SUB):
                    s = inv[k][0] * cols[0]
                    for m in range(1, k + 1):
                        s = s + inv[k][m] * cols[m]
                    cq.append(s)
                panels[q] = panels[q] - rows_times(cq, u)
            yield
        r1 = r0 + BLK
        if r1 < n:
            ub = u_ref[r0:r1, :]
            m_ref[r1:, :] = m_ref[r1:, :] - lax.dot_general(
                ub[:, r1:n], ub, (((0,), (0,)), ((), ())), precision=HIGHEST, preferred_element_type=jnp.float32)


def peak_of(x):
    rows = jnp.max(jnp.abs(x).reshape(-1, 16, x.shape[1]), axis=0).astype(jnp.float32)
    return jnp.max(rows)


def power_kernel(steps, slab, scale, bound, job, flags_ref, a_ref, g_ref, b_ref, out_ref, acc_ref, peak_ref):
    t = pl.program_id(0)

    @pl.when(t == 0)
    def _():
        acc_ref[...] = jnp.zeros_like(acc_ref)
        peak_ref[0] = 0.0
        peak_ref[1] = 0.0

    peak_ref[0] = jnp.maximum(peak_ref[0], peak_of(a_ref[...]))
    peak_ref[1] = jnp.maximum(peak_ref[1], peak_of(g_ref[...]))

    def add(x):
        proj = jnp.dot(x, b_ref[0], preferred_element_type=jnp.float32).astype(jnp.bfloat16)
        acc_ref[...] += lax.dot_general(proj, x, TOP, preferred_element_type=jnp.float32)

    @pl.when(job(flags_ref) == 0)
    def _():
        add(a_ref[...])

    @pl.when(job(flags_ref) != 0)
    def _():
        add(g_ref[...])

    @pl.when(t == steps - 1)
    def _():
        out = acc_ref[...].T * scale
        row = (1, 1, out.shape[1])
        power = exponent(jnp.full(row, jnp.max(jnp.abs(out)), jnp.float32))
        out_ref[:, :slab] = out.reshape(-1, slab, out.shape[1]) * jnp.exp2(power)
        grad = exponent(jnp.full(row, peak_ref[0] * peak_ref[1] * bound, jnp.float32))
        shape = (out_ref.shape[0], EDGE, out.shape[1])
        out_ref[:, slab:] = jnp.where(lax.broadcasted_iota(jnp.int32, shape, 1) == 0, power, grad)


def job_of(flags):
    column = lax.axis_index("mp") + 1
    return jnp.where(jnp.where(column == 1, flags[1], flags[2]) == 1, column, 0)


def local_power(flags, a, g, basis, slab, total_tokens):
    tokens, width = a.shape
    rank = basis.shape[2]
    tile = 512
    steps = tokens // tile
    out = jax.ShapeDtypeStruct((width // slab, slab + EDGE, rank), jnp.float32)
    bound = tokens / math.sqrt(total_tokens)
    return pl.pallas_call(
        functools.partial(power_kernel, steps, slab, 1.0 / total_tokens, bound, job_of),
        out_shape=out,
        grid_spec=pltpu.PrefetchScalarGridSpec(
            num_scalar_prefetch=1,
            grid=(steps,),
            in_specs=[
                pl.BlockSpec((tile, width), lambda t, s: (t, 0)),
                pl.BlockSpec((tile, width), lambda t, s: (t, 0)),
                pl.BlockSpec((1, width, rank), lambda t, f: (job_of(f), 0, 0)),
            ],
            out_specs=pl.BlockSpec(out.shape, lambda t, s: (0, 0, 0)),
            scratch_shapes=[pltpu.VMEM((rank, width), jnp.float32), pltpu.SMEM((2,), jnp.float32)],
        ),
        compiler_params=pltpu.CompilerParams(vmem_limit_bytes=VMEM_BYTES),
        cost_estimate=BRIEF,
        name="local_power",
    )(flags, a, g, basis)


def grad_kernel(scale, s_ref, a_ref, ao_ref, g_ref, go_ref, out_ref):
    rows = 256
    slabs = rows // out_ref.shape[1]
    for part in range(a_ref.shape[1] // rows):
        cut = slice(part * rows, (part + 1) * rows)
        out = lax.dot_general(a_ref[:, cut], g_ref[...], TOP, preferred_element_type=jnp.float32)
        out += lax.dot_general(ao_ref[:, cut], go_ref[...], TOP, preferred_element_type=jnp.float32)
        out_ref[part * slabs:(part + 1) * slabs] = (scale * out).reshape(slabs, *out_ref.shape[1:])


def pair_grad(scalars, a, a_other, g, g_other, slab, scale):
    tokens, width = a.shape
    cols = g_other.shape[1]
    rows = 512
    return pl.pallas_call(
        functools.partial(grad_kernel, scale),
        out_shape=jax.ShapeDtypeStruct((width // slab, slab, cols), jnp.float32),
        grid_spec=pltpu.PrefetchScalarGridSpec(
            num_scalar_prefetch=1,
            grid=(width // rows,),
            in_specs=[
                pl.BlockSpec((tokens, rows), lambda i, s: (0, i)),
                pl.BlockSpec((tokens, rows), lambda i, s: (0, i)),
                pl.BlockSpec((tokens, cols), lambda i, s: (0, s[1])),
                pl.BlockSpec((tokens, cols), lambda i, s: (0, 0)),
            ],
            out_specs=pl.BlockSpec((rows // slab, slab, cols), lambda i, s: (i, 0, 0)),
        ),
        compiler_params=pltpu.CompilerParams(vmem_limit_bytes=VMEM_BYTES),
        cost_estimate=BRIEF,
        name="pair_grad",
    )(scalars, a, a_other, g, g_other)


def parts_of(x):
    high = x.astype(jnp.bfloat16)
    return high, (x - high.astype(jnp.float32)).astype(jnp.bfloat16)


def bf16_dot(x, y, dims):
    return lax.dot_general(x, y, dims, preferred_element_type=jnp.float32)


def gather_kernel(slab, got_ref, out_ref, power_ref, up_ref, down_ref):
    powers = got_ref[:, slab:slab + 1]
    rows = jnp.sum(got_ref[:, :slab] * jnp.exp2(-powers), axis=0)
    power = exponent(jnp.sum(jnp.exp2(15.0 - powers), axis=0))
    out_ref[...] = rows * jnp.exp2(power)
    power_ref[...] = jnp.broadcast_to(power, power_ref.shape)
    least = jnp.full(up_ref.shape, jnp.min(got_ref[:, slab + 1:slab + 2]) - 1.0, jnp.float32)
    up_ref[...] = jnp.exp2(least)
    down_ref[...] = jnp.exp2(-least)


def sum_rows(got, slab, width):
    line = jax.ShapeDtypeStruct((SUB, width), jnp.float32)
    rank = got.shape[2]
    return pl.pallas_call(
        functools.partial(gather_kernel, slab),
        out_shape=(
            jax.ShapeDtypeStruct((slab, rank), jnp.float32),
            jax.ShapeDtypeStruct((SUB, rank), jnp.float32),
            line,
            line,
        ),
        compiler_params=pltpu.CompilerParams(vmem_limit_bytes=VMEM_BYTES),
        cost_estimate=BRIEF,
        name="sum_rows",
    )(got)


def factor_kernel(
    s_ref, near_ref, far_ref, pa_ref, pg_ref, wa_ref, wg_ref, ea_ref, eg_ref, ma_ref, ua_ref, mg_ref, ug_ref
):
    n = wa_ref.shape[0]
    core = s_ref[1]
    eye = lax.broadcasted_iota(jnp.int32, (n, n), 0) == lax.broadcasted_iota(jnp.int32, (n, n), 1)
    for place, p_ref, m_ref in ((5, pa_ref, ma_ref), (6, pg_ref, mg_ref)):
        for got_ref, slot in ((near_ref, core), (far_ref, 1 - core)):
            p_ref[:, slot] = got_ref[:, s_ref[place]]
        p = p_ref[...].reshape(-1, n)
        high, low = parts_of(p)
        cross = bf16_dot(high, low, TOP)
        m_ref[:, :n] = bf16_dot(high, high, TOP) + ((cross + cross.T) + bf16_dot(low, low, TOP))
        m_ref[:, n:] = eye.astype(jnp.float32)
    for _ in zip(factor_steps(ma_ref, ua_ref), factor_steps(mg_ref, ug_ref), strict=True):
        pass
    for u_ref, w_ref, e_ref in ((ua_ref, wa_ref, ea_ref), (ug_ref, wg_ref, eg_ref)):
        w_ref[...] = u_ref[:, n:]
        eig = jnp.sum(jnp.where(eye, u_ref[:, :n], 0.0), axis=0, keepdims=True)
        e_ref[...] = jnp.broadcast_to(eig, (SUB, n))


def factor_powers(scalars, near, far):
    chips, slab, n = near.shape[0], near.shape[2], near.shape[3]
    square = jax.ShapeDtypeStruct((n, n), jnp.float32)
    row = jax.ShapeDtypeStruct((SUB, n), jnp.float32)
    tall = jax.ShapeDtypeStruct((chips, 2, slab, n), jnp.float32)
    vmem = pl.BlockSpec(memory_space=pltpu.VMEM)
    return pl.pallas_call(
        factor_kernel,
        out_shape=(tall, tall, square, square, row, row),
        in_specs=[pl.BlockSpec(memory_space=pltpu.SMEM), vmem, vmem],
        out_specs=(vmem,) * 6,
        scratch_shapes=[pltpu.VMEM((n, 2 * n), jnp.float32)] * 4,
        compiler_params=pltpu.CompilerParams(vmem_limit_bytes=VMEM_BYTES),
        cost_estimate=BRIEF,
        name="factor_powers",
    )(scalars, near, far)


def core_kernel(scale, s_ref, a_ref, g_ref, pa_ref, pg_ref, wa_ref, wg_ref, oa_ref, og_ref, ba_ref, bg_ref, core_ref):
    t = pl.program_id(0)

    @pl.when(t == 0)
    def _():
        core_ref[...] = jnp.zeros_like(core_ref)
        for place, p_ref, w_ref, old_ref, b_ref in (
            (2, pa_ref, wa_ref, oa_ref, ba_ref),
            (3, pg_ref, wg_ref, og_ref, bg_ref),
        ):
            @pl.when(s_ref[place] == 1)
            def _():
                p_high, p_low = parts_of(p_ref[...])
                w_high, w_low = parts_of(w_ref[...])
                fresh = bf16_dot(p_high, w_high, LAST) + (bf16_dot(p_high, w_low, LAST) + bf16_dot(p_low, w_high, LAST))
                b_ref[...] = fresh.astype(jnp.bfloat16)

            @pl.when(s_ref[place] != 1)
            def _():
                b_ref[...] = old_ref[0]

    left = jnp.dot(a_ref[...], ba_ref[...], preferred_element_type=jnp.float32)
    right = jnp.dot(g_ref[...], bg_ref[...], preferred_element_type=jnp.float32)
    core_ref[...] += scale * lax.dot_general(
        left, right, TOP, precision=HIGHEST, preferred_element_type=jnp.float32
    )


def core_part(scalars, a, g, power_a, power_g, w_a, w_g, old_basis, scale):
    tokens, width = a.shape
    rank = w_a.shape[0]
    tile = 512
    tall = pl.BlockSpec((width, rank), lambda t, s: (0, 0))
    square = pl.BlockSpec((rank, rank), lambda t, s: (0, 0))
    return pl.pallas_call(
        functools.partial(core_kernel, scale),
        out_shape=(
            jax.ShapeDtypeStruct((width, rank), jnp.bfloat16),
            jax.ShapeDtypeStruct((width, rank), jnp.bfloat16),
            jax.ShapeDtypeStruct((rank, rank), jnp.float32),
        ),
        grid_spec=pltpu.PrefetchScalarGridSpec(
            num_scalar_prefetch=1,
            grid=(tokens // tile,),
            in_specs=[
                pl.BlockSpec((tile, width), lambda t, s: (t, 0)),
                pl.BlockSpec((tile, width), lambda t, s: (t, 0)),
                tall,
                tall,
                square,
                square,
                pl.BlockSpec((1, width, rank), lambda t, s: (0, 0, 0)),
                pl.BlockSpec((1, width, rank), lambda t, s: (s[4], 0, 0)),
            ],
            out_specs=(tall, tall, square),
        ),
        compiler_params=pltpu.CompilerParams(vmem_limit_bytes=VMEM_BYTES),
        cost_estimate=BRIEF,
        name="core_part",
    )(scalars, a, g, power_a, power_g, w_a, w_g, old_basis, old_basis)


def swap(x, axis):
    return lax.ppermute(x, axis, [(0, 1), (1, 0)])


def exponent(bound):
    return jnp.floor(15.0 - jnp.log2(jnp.maximum(bound, 2.0**-100)))


def body(activations, out_grads, old_basis, old_eigen, flags):
    tok_rows, width = activations.shape
    rank = old_basis.shape[2]
    dp_count = lax.axis_size(DP)
    chips = dp_count // 2
    total_tokens = tok_rows * dp_count
    slab_rows = width // dp_count
    scale = 1.0 / math.sqrt(total_tokens)
    row_start = lax.axis_index(DP) * slab_rows
    core_id = lax.axis_index("c")
    mp_id = lax.axis_index("mp")
    column = mp_id + 1
    flag_a = flags[0]
    flag_g = jnp.where(mp_id == 0, flags[1], flags[2])

    source_a = jnp.where(flags[1] == 1, 1, 0)
    job = jnp.where(flag_g == 1, column, 0)
    place = lax.iota(jnp.int32, 8)
    scalars = jnp.zeros(8, jnp.int32)
    for index, value in enumerate((job, core_id, flag_a, flag_g, column, source_a, mp_id)):
        scalars = jnp.where(place == index, value, scalars)
    cols = width // 2
    give = lax.dynamic_slice_in_dim(out_grads, (1 - core_id) * cols, cols, 1)
    give, out_grads = lax.optimization_barrier((give, out_grads))
    a_other, g_other = swap(activations, "c"), swap(give, "c")
    half = local_power(flags, activations, out_grads, old_basis, slab_rows, total_tokens).astype(jnp.float16)
    half, activations = lax.optimization_barrier((half, activations))
    got = lax.all_to_all(half, DP, 0, 0, tiled=True)
    grad = pair_grad(scalars, activations, a_other, out_grads, g_other, 2 * slab_rows, scale)
    got, grad = lax.optimization_barrier((got, grad))
    spread, own, up, down = sum_rows(got.astype(jnp.float32), slab_rows, cols)
    spread = jnp.broadcast_to(spread.astype(jnp.float16), (2 * chips, slab_rows, rank))
    spread, grad = lax.optimization_barrier((spread, grad))
    near = lax.all_to_all(spread, CHIPS + ("mp",), 0, 0, tiled=True)
    half = (grad * up[:1]).astype(jnp.float16)
    near, half = lax.optimization_barrier((near, half))
    far = swap(near, "c")
    got = lax.all_to_all(half, CHIPS, 0, 0, tiled=True)

    both = (chips, 2, slab_rows, rank)
    power_a, power_g, w_a, w_g, root_a, root_g = factor_powers(
        scalars, near.astype(jnp.float32).reshape(both), far.astype(jnp.float32).reshape(both)
    )
    own, w_g = lax.optimization_barrier((own, w_g))
    other = swap(own, "mp")
    power_a, power_g = power_a.reshape(width, rank), power_g.reshape(width, rank)
    basis_a, basis_g, core = core_part(
        scalars, activations, out_grads, power_a, power_g, w_a, w_g, old_basis, scale
    )
    got, core, other = lax.optimization_barrier((got, core, other))
    part = rank // dp_count
    core = core.astype(jnp.bfloat16).reshape(dp_count, part, rank)
    core = lax.all_to_all(core, DP, 0, 0, tiled=True)
    grad = jnp.sum(got.astype(jnp.float32), axis=0) * down[:1]
    near = lax.dynamic_slice_in_dim(grad, core_id * slab_rows, slab_rows, 0)
    give = lax.dynamic_slice_in_dim(grad, (1 - core_id) * slab_rows, slab_rows, 0)
    near, give, core = lax.optimization_barrier((near, give, core))
    far = swap(give, "c")
    core = lax.optimization_barrier(jnp.sum(core.astype(jnp.float32), axis=0))
    core = jnp.broadcast_to(core.astype(jnp.bfloat16), (dp_count, part, rank))
    core = lax.all_to_all(core, DP, 0, 0, tiled=True).astype(jnp.float32).reshape(rank, rank)
    grad_rows = jnp.where(
        core_id == 0, jnp.concatenate([near, far], axis=1), jnp.concatenate([far, near], axis=1)
    )

    power_a = jnp.where(source_a == mp_id, own[0], other[0])
    eig_a = jnp.where(flag_a == 1, root_a[0] * jnp.exp2(-power_a), old_eigen[0])
    eigen_g = lax.dynamic_index_in_dim(old_eigen, column, 0, keepdims=False)
    eig_g = jnp.where(flag_g == 1, root_g[0] * jnp.exp2(-own[0]), eigen_g)
    damping = jnp.mean(eig_a) * jnp.mean(eig_g)
    outer = eig_a[:, None] * eig_g[None, :]
    weight = outer / (outer + damping)
    wide_a = lax.dynamic_slice_in_dim(basis_a, row_start, slab_rows, 0).astype(jnp.float32)
    wide_g = basis_g.astype(jnp.float32)
    left = jnp.dot(wide_a, weight * core, precision=HIGHEST)
    correction = jnp.einsum("ir,kr->ik", left, wide_g, precision=HIGHEST)
    return grad_rows - correction


def solution(mesh):
    split = Mesh(mesh.devices.reshape(4, 4, 2, 2, 2), ("y", "x", "z", "c", "mp"))
    placed = (P(DP, None), P(DP, "mp"), P(), P(), P())
    return jax.shard_map(body, mesh=split, in_specs=placed, out_specs=P(DP, "mp"), check_vma=False)
```

```python
import functools
import math

import jax
import jax.numpy as jnp
from jax import lax
from jax.experimental import pallas as pl
from jax.experimental.pallas import tpu as pltpu
from jax.sharding import Mesh, PartitionSpec as P

DP = ("y", "x", "z", "c")
CHIPS = ("y", "x", "z")
HIGHEST = lax.Precision.HIGHEST
TOP = (((0,), (0,)), ((), ()))
LAST = (((1,), (1,)), ((), ()))
BLK = 32
SUB = 8
EDGE = 8
VMEM_BYTES = 50 << 20
BRIEF = pl.CostEstimate(flops=1_000_000, bytes_accessed=10_000, transcendentals=0)


def small_factor(cols):
    shape = cols[0].shape
    e = [[jnp.broadcast_to(cols[k][i:i + 1, :], shape) for k in range(i + 1)] for i in range(SUB)]
    low = [[None] * SUB for _ in range(SUB)]
    rinv = []
    for j in range(SUB):
        d = e[j][j]
        r = lax.rsqrt(d)
        r = r * (1.5 - 0.5 * d * r * r)
        rinv.append(r)
        for i in range(j + 1, SUB):
            low[i][j] = e[i][j] * r
        for i in range(j + 1, SUB):
            for k in range(j + 1, i + 1):
                e[i][k] = e[i][k] - low[i][j] * low[k][j]
    inv = [[None] * SUB for _ in range(SUB)]
    for k in range(SUB):
        inv[k][k] = rinv[k]
        for i in range(k + 1, SUB):
            s = low[i][k] * inv[k][k]
            for m in range(k + 1, i):
                s = s + low[i][m] * inv[m][k]
            inv[i][k] = -s * rinv[i]
    return inv


def lane_splat(x, col):
    return jnp.broadcast_to(x[:, col:col + 1], (SUB, 128))


def rows_times(coefs, rows):
    n = rows.shape[1]
    out = []
    for g in range(n // 128):
        t = rows[:, g * 128:(g + 1) * 128]
        prods = [coefs[k] * jnp.broadcast_to(t[k:k + 1, :], (SUB, 128)) for k in range(SUB)]
        while len(prods) > 1:
            prods = [a + b for a, b in zip(prods[::2], prods[1::2])]
        out.append(prods[0])
    return jnp.concatenate(out, axis=1)


def factor_steps(m_ref, u_ref):
    n = m_ref.shape[0]
    sub = lax.broadcasted_iota(jnp.int32, (SUB, 128), 0)
    for r0 in range(0, n, BLK):
        panels = [m_ref[r0 + SUB * p:r0 + SUB * (p + 1), :] for p in range(BLK // SUB)]
        for p in range(BLK // SUB):
            c0 = r0 + SUB * p
            inv = small_factor([lane_splat(panels[p], c0 + m) for m in range(SUB)])
            coefs = []
            for k in range(SUB):
                v = jnp.zeros((SUB, 128), jnp.float32)
                for i in range(k, SUB):
                    v = jnp.where(sub == i, inv[i][k], v)
                coefs.append(v)
            u = rows_times(coefs, panels[p])
            u_ref[c0:c0 + SUB, :] = u
            for q in range(p + 1, BLK // SUB):
                cols = [lane_splat(panels[q], c0 + m) for m in range(SUB)]
                cq = []
                for k in range(SUB):
                    s = inv[k][0] * cols[0]
                    for m in range(1, k + 1):
                        s = s + inv[k][m] * cols[m]
                    cq.append(s)
                panels[q] = panels[q] - rows_times(cq, u)
            yield
        r1 = r0 + BLK
        if r1 < n:
            ub = u_ref[r0:r1, :]
            m_ref[r1:, :] = m_ref[r1:, :] - lax.dot_general(
                ub[:, r1:n], ub, (((0,), (0,)), ((), ())), precision=HIGHEST, preferred_element_type=jnp.float32)


def peak_of(x):
    rows = jnp.max(jnp.abs(x).reshape(-1, 16, x.shape[1]), axis=0).astype(jnp.float32)
    return jnp.max(rows)


def power_kernel(steps, slab, scale, bound, job, flags_ref, a_ref, g_ref, b_ref, out_ref, acc_ref, peak_ref):
    t = pl.program_id(0)

    @pl.when(t == 0)
    def _():
        acc_ref[...] = jnp.zeros_like(acc_ref)
        peak_ref[0] = 0.0
        peak_ref[1] = 0.0

    peak_ref[0] = jnp.maximum(peak_ref[0], peak_of(a_ref[...]))
    peak_ref[1] = jnp.maximum(peak_ref[1], peak_of(g_ref[...]))

    def add(x):
        proj = jnp.dot(x, b_ref[0], preferred_element_type=jnp.float32).astype(jnp.bfloat16)
        acc_ref[...] += lax.dot_general(proj, x, TOP, preferred_element_type=jnp.float32)

    @pl.when(job(flags_ref) == 0)
    def _():
        add(a_ref[...])

    @pl.when(job(flags_ref) != 0)
    def _():
        add(g_ref[...])

    @pl.when(t == steps - 1)
    def _():
        out = acc_ref[...].T * scale
        row = (1, 1, out.shape[1])
        power = exponent(jnp.full(row, jnp.max(jnp.abs(out)), jnp.float32))
        out_ref[:, :slab] = out.reshape(-1, slab, out.shape[1]) * jnp.exp2(power)
        grad = exponent(jnp.full(row, peak_ref[0] * peak_ref[1] * bound, jnp.float32))
        shape = (out_ref.shape[0], EDGE, out.shape[1])
        out_ref[:, slab:] = jnp.where(lax.broadcasted_iota(jnp.int32, shape, 1) == 0, power, grad)


def job_of(flags):
    column = lax.axis_index("mp") + 1
    return jnp.where(jnp.where(column == 1, flags[1], flags[2]) == 1, column, 0)


def local_power(flags, a, g, basis, slab, total_tokens):
    tokens, width = a.shape
    rank = basis.shape[2]
    tile = 512
    steps = tokens // tile
    out = jax.ShapeDtypeStruct((width // slab, slab + EDGE, rank), jnp.float32)
    bound = tokens / math.sqrt(total_tokens)
    return pl.pallas_call(
        functools.partial(power_kernel, steps, slab, 1.0 / total_tokens, bound, job_of),
        out_shape=out,
        grid_spec=pltpu.PrefetchScalarGridSpec(
            num_scalar_prefetch=1,
            grid=(steps,),
            in_specs=[
                pl.BlockSpec((tile, width), lambda t, s: (t, 0)),
                pl.BlockSpec((tile, width), lambda t, s: (t, 0)),
                pl.BlockSpec((1, width, rank), lambda t, f: (job_of(f), 0, 0)),
            ],
            out_specs=pl.BlockSpec(out.shape, lambda t, s: (0, 0, 0)),
            scratch_shapes=[pltpu.VMEM((rank, width), jnp.float32), pltpu.SMEM((2,), jnp.float32)],
        ),
        compiler_params=pltpu.CompilerParams(vmem_limit_bytes=VMEM_BYTES),
        cost_estimate=BRIEF,
        name="local_power",
    )(flags, a, g, basis)


def grad_kernel(scale, a_ref, ao_ref, g_ref, go_ref, out_ref):
    rows = 256
    slabs = rows // out_ref.shape[1]
    for part in range(a_ref.shape[1] // rows):
        cut = slice(part * rows, (part + 1) * rows)
        out = lax.dot_general(a_ref[:, cut], g_ref[...], TOP, preferred_element_type=jnp.float32)
        out += lax.dot_general(ao_ref[:, cut], go_ref[...], TOP, preferred_element_type=jnp.float32)
        out_ref[part * slabs:(part + 1) * slabs] = (scale * out).reshape(slabs, *out_ref.shape[1:])


def pair_grad(a, a_other, g, g_other, slab, scale):
    tokens, width = a.shape
    cols = g_other.shape[1]
    rows = 512
    return pl.pallas_call(
        functools.partial(grad_kernel, scale),
        out_shape=jax.ShapeDtypeStruct((width // slab, slab, cols), jnp.float32),
        grid=(width // rows,),
        in_specs=[
            pl.BlockSpec((tokens, rows), lambda i: (0, i)),
            pl.BlockSpec((tokens, rows), lambda i: (0, i)),
            pl.BlockSpec((tokens, cols), lambda i: (0, lax.axis_index("c"))),
            pl.BlockSpec((tokens, cols), lambda i: (0, 0)),
        ],
        out_specs=pl.BlockSpec((rows // slab, slab, cols), lambda i: (i, 0, 0)),
        compiler_params=pltpu.CompilerParams(vmem_limit_bytes=VMEM_BYTES),
        cost_estimate=BRIEF,
        name="pair_grad",
    )(a, a_other, g, g_other)


def copy_kernel(x_ref, out_ref):
    out_ref[...] = x_ref[...]


def other_half(x):
    tokens, width = x.shape
    cols = width // 2
    tile = 256
    return pl.pallas_call(
        copy_kernel,
        out_shape=jax.ShapeDtypeStruct((tokens, cols), x.dtype),
        grid=(tokens // tile,),
        in_specs=[pl.BlockSpec((tile, cols), lambda t: (t, 1 - lax.axis_index("c")))],
        out_specs=pl.BlockSpec((tile, cols), lambda t: (t, 0)),
        compiler_params=pltpu.CompilerParams(vmem_limit_bytes=VMEM_BYTES),
        cost_estimate=BRIEF,
        name="other_half",
    )(x)


def parts_of(x):
    high = x.astype(jnp.bfloat16)
    return high, (x - high.astype(jnp.float32)).astype(jnp.bfloat16)


def bf16_dot(x, y, dims):
    return lax.dot_general(x, y, dims, preferred_element_type=jnp.float32)


def gather_kernel(slab, got_ref, out_ref, power_ref, up_ref, down_ref):
    powers = got_ref[:, slab:slab + 1]
    rows = jnp.sum(got_ref[:, :slab] * jnp.exp2(-powers), axis=0)
    power = exponent(jnp.sum(jnp.exp2(15.0 - powers), axis=0))
    out_ref[...] = rows * jnp.exp2(power)
    power_ref[...] = jnp.broadcast_to(power, power_ref.shape)
    least = jnp.full(up_ref.shape, jnp.min(got_ref[:, slab + 1:slab + 2]) - 1.0, jnp.float32)
    up_ref[...] = jnp.exp2(least)
    down_ref[...] = jnp.exp2(-least)


def sum_rows(got, slab, width):
    line = jax.ShapeDtypeStruct((SUB, width), jnp.float32)
    rank = got.shape[2]
    return pl.pallas_call(
        functools.partial(gather_kernel, slab),
        out_shape=(
            jax.ShapeDtypeStruct((slab, rank), jnp.float32),
            jax.ShapeDtypeStruct((SUB, rank), jnp.float32),
            line,
            line,
        ),
        compiler_params=pltpu.CompilerParams(vmem_limit_bytes=VMEM_BYTES),
        cost_estimate=BRIEF,
        name="sum_rows",
    )(got)


def factor_kernel(
    s_ref, near_ref, far_ref, pa_ref, pg_ref, wa_ref, wg_ref, ea_ref, eg_ref, ma_ref, ua_ref, mg_ref, ug_ref
):
    n = wa_ref.shape[0]
    core = s_ref[1]
    eye = lax.broadcasted_iota(jnp.int32, (n, n), 0) == lax.broadcasted_iota(jnp.int32, (n, n), 1)
    for place, p_ref, m_ref in ((5, pa_ref, ma_ref), (6, pg_ref, mg_ref)):
        for got_ref, slot in ((near_ref, core), (far_ref, 1 - core)):
            p_ref[:, slot] = got_ref[:, s_ref[place]]
        p = p_ref[...].reshape(-1, n)
        high, low = parts_of(p)
        cross = bf16_dot(high, low, TOP)
        m_ref[:, :n] = bf16_dot(high, high, TOP) + ((cross + cross.T) + bf16_dot(low, low, TOP))
        m_ref[:, n:] = eye.astype(jnp.float32)
    for _ in zip(factor_steps(ma_ref, ua_ref), factor_steps(mg_ref, ug_ref), strict=True):
        pass
    for u_ref, w_ref, e_ref in ((ua_ref, wa_ref, ea_ref), (ug_ref, wg_ref, eg_ref)):
        w_ref[...] = u_ref[:, n:]
        eig = jnp.sum(jnp.where(eye, u_ref[:, :n], 0.0), axis=0, keepdims=True)
        e_ref[...] = jnp.broadcast_to(eig, (SUB, n))


def factor_powers(scalars, near, far):
    chips, slab, n = near.shape[0], near.shape[2], near.shape[3]
    square = jax.ShapeDtypeStruct((n, n), jnp.float32)
    row = jax.ShapeDtypeStruct((SUB, n), jnp.float32)
    tall = jax.ShapeDtypeStruct((chips, 2, slab, n), jnp.float32)
    vmem = pl.BlockSpec(memory_space=pltpu.VMEM)
    return pl.pallas_call(
        factor_kernel,
        out_shape=(tall, tall, square, square, row, row),
        in_specs=[pl.BlockSpec(memory_space=pltpu.SMEM), vmem, vmem],
        out_specs=(vmem,) * 6,
        scratch_shapes=[pltpu.VMEM((n, 2 * n), jnp.float32)] * 4,
        compiler_params=pltpu.CompilerParams(vmem_limit_bytes=VMEM_BYTES),
        cost_estimate=BRIEF,
        name="factor_powers",
    )(scalars, near, far)


def core_kernel(scale, s_ref, a_ref, g_ref, pa_ref, pg_ref, wa_ref, wg_ref, oa_ref, og_ref, ba_ref, bg_ref, core_ref):
    t = pl.program_id(0)

    @pl.when(t == 0)
    def _():
        core_ref[...] = jnp.zeros_like(core_ref)
        for place, p_ref, w_ref, old_ref, b_ref in (
            (2, pa_ref, wa_ref, oa_ref, ba_ref),
            (3, pg_ref, wg_ref, og_ref, bg_ref),
        ):
            @pl.when(s_ref[place] == 1)
            def _():
                p_high, p_low = parts_of(p_ref[...])
                w_high, w_low = parts_of(w_ref[...])
                fresh = bf16_dot(p_high, w_high, LAST) + (bf16_dot(p_high, w_low, LAST) + bf16_dot(p_low, w_high, LAST))
                b_ref[...] = fresh.astype(jnp.bfloat16)

            @pl.when(s_ref[place] != 1)
            def _():
                b_ref[...] = old_ref[0]

    left = jnp.dot(a_ref[...], ba_ref[...], preferred_element_type=jnp.float32)
    right = jnp.dot(g_ref[...], bg_ref[...], preferred_element_type=jnp.float32)
    core_ref[...] += scale * lax.dot_general(
        left, right, TOP, precision=HIGHEST, preferred_element_type=jnp.float32
    )


def core_part(scalars, a, g, power_a, power_g, w_a, w_g, old_basis, scale):
    tokens, width = a.shape
    rank = w_a.shape[0]
    tile = 512
    tall = pl.BlockSpec((width, rank), lambda t, s: (0, 0))
    square = pl.BlockSpec((rank, rank), lambda t, s: (0, 0))
    return pl.pallas_call(
        functools.partial(core_kernel, scale),
        out_shape=(
            jax.ShapeDtypeStruct((width, rank), jnp.bfloat16),
            jax.ShapeDtypeStruct((width, rank), jnp.bfloat16),
            jax.ShapeDtypeStruct((rank, rank), jnp.float32),
        ),
        grid_spec=pltpu.PrefetchScalarGridSpec(
            num_scalar_prefetch=1,
            grid=(tokens // tile,),
            in_specs=[
                pl.BlockSpec((tile, width), lambda t, s: (t, 0)),
                pl.BlockSpec((tile, width), lambda t, s: (t, 0)),
                tall,
                tall,
                square,
                square,
                pl.BlockSpec((1, width, rank), lambda t, s: (0, 0, 0)),
                pl.BlockSpec((1, width, rank), lambda t, s: (s[4], 0, 0)),
            ],
            out_specs=(tall, tall, square),
        ),
        compiler_params=pltpu.CompilerParams(vmem_limit_bytes=VMEM_BYTES),
        cost_estimate=BRIEF,
        name="core_part",
    )(scalars, a, g, power_a, power_g, w_a, w_g, old_basis, old_basis)


def swap(x, axis):
    return lax.ppermute(x, axis, [(0, 1), (1, 0)])


def exponent(bound):
    return jnp.floor(15.0 - jnp.log2(jnp.maximum(bound, 2.0**-100)))


def body(activations, out_grads, old_basis, old_eigen, flags):
    tok_rows, width = activations.shape
    rank = old_basis.shape[2]
    dp_count = lax.axis_size(DP)
    chips = dp_count // 2
    total_tokens = tok_rows * dp_count
    slab_rows = width // dp_count
    scale = 1.0 / math.sqrt(total_tokens)
    row_start = lax.axis_index(DP) * slab_rows
    core_id = lax.axis_index("c")
    mp_id = lax.axis_index("mp")
    column = mp_id + 1
    flag_a = flags[0]
    flag_g = jnp.where(mp_id == 0, flags[1], flags[2])

    source_a = jnp.where(flags[1] == 1, 1, 0)
    job = jnp.where(flag_g == 1, column, 0)
    place = lax.iota(jnp.int32, 8)
    scalars = jnp.zeros(8, jnp.int32)
    for index, value in enumerate((job, core_id, flag_a, flag_g, column, source_a, mp_id)):
        scalars = jnp.where(place == index, value, scalars)
    cols = width // 2
    give = other_half(out_grads)
    give, out_grads = lax.optimization_barrier((give, out_grads))
    a_other, g_other = swap(activations, "c"), swap(give, "c")
    half = local_power(flags, activations, out_grads, old_basis, slab_rows, total_tokens).astype(jnp.float16)
    half, activations = lax.optimization_barrier((half, activations))
    got = lax.all_to_all(half, DP, 0, 0, tiled=True)
    grad = pair_grad(activations, a_other, out_grads, g_other, 2 * slab_rows, scale)
    got, grad = lax.optimization_barrier((got, grad))
    spread, own, up, down = sum_rows(got.astype(jnp.float32), slab_rows, cols)
    spread = jnp.broadcast_to(spread.astype(jnp.float16), (2 * chips, slab_rows, rank))
    spread, grad = lax.optimization_barrier((spread, grad))
    near = lax.all_to_all(spread, CHIPS + ("mp",), 0, 0, tiled=True)
    half = (grad * up[:1]).astype(jnp.float16)
    near, half = lax.optimization_barrier((near, half))
    far = swap(near, "c")
    got = lax.all_to_all(half, CHIPS, 0, 0, tiled=True)

    both = (chips, 2, slab_rows, rank)
    power_a, power_g, w_a, w_g, root_a, root_g = factor_powers(
        scalars, near.astype(jnp.float32).reshape(both), far.astype(jnp.float32).reshape(both)
    )
    own, w_g = lax.optimization_barrier((own, w_g))
    other = swap(own, "mp")
    power_a, power_g = power_a.reshape(width, rank), power_g.reshape(width, rank)
    basis_a, basis_g, core = core_part(
        scalars, activations, out_grads, power_a, power_g, w_a, w_g, old_basis, scale
    )
    got, core, other = lax.optimization_barrier((got, core, other))
    part = rank // dp_count
    core = core.astype(jnp.bfloat16).reshape(dp_count, part, rank)
    core = lax.all_to_all(core, DP, 0, 0, tiled=True)
    grad = jnp.sum(got.astype(jnp.float32), axis=0) * down[:1]
    near = lax.dynamic_slice_in_dim(grad, core_id * slab_rows, slab_rows, 0)
    give = lax.dynamic_slice_in_dim(grad, (1 - core_id) * slab_rows, slab_rows, 0)
    near, give, core = lax.optimization_barrier((near, give, core))
    far = swap(give, "c")
    core = lax.optimization_barrier(jnp.sum(core.astype(jnp.float32), axis=0))
    core = jnp.broadcast_to(core.astype(jnp.bfloat16), (dp_count, part, rank))
    core = lax.all_to_all(core, DP, 0, 0, tiled=True).astype(jnp.float32).reshape(rank, rank)
    grad_rows = jnp.where(
        core_id == 0, jnp.concatenate([near, far], axis=1), jnp.concatenate([far, near], axis=1)
    )

    power_a = jnp.where(source_a == mp_id, own[0], other[0])
    eig_a = jnp.where(flag_a == 1, root_a[0] * jnp.exp2(-power_a), old_eigen[0])
    eigen_g = lax.dynamic_index_in_dim(old_eigen, column, 0, keepdims=False)
    eig_g = jnp.where(flag_g == 1, root_g[0] * jnp.exp2(-own[0]), eigen_g)
    damping = jnp.mean(eig_a) * jnp.mean(eig_g)
    outer = eig_a[:, None] * eig_g[None, :]
    weight = outer / (outer + damping)
    wide_a = lax.dynamic_slice_in_dim(basis_a, row_start, slab_rows, 0).astype(jnp.float32)
    wide_g = basis_g.astype(jnp.float32)
    left = jnp.dot(wide_a, weight * core, precision=HIGHEST)
    correction = jnp.einsum("ir,kr->ik", left, wide_g, precision=HIGHEST)
    return grad_rows - correction


def solution(mesh):
    split = Mesh(mesh.devices.reshape(4, 4, 2, 2, 2), ("y", "x", "z", "c", "mp"))
    placed = (P(DP, None), P(DP, "mp"), P(), P(), P())
    return jax.shard_map(body, mesh=split, in_specs=placed, out_specs=P(DP, "mp"), check_vma=False)
```
